32 devices in a mesh: blk: 8 (over y, x, core), req: 4 (over z).
Axes of the slice: x: 2, y: 2, z: 4, core: 2. Of those that a mesh axis runs over, the one named last changes fastest.
Arguments:
- long_q: bfloat16 [8192, 2048], P('blk', 'req'), may hold values from -6 to 6
- long_k: bfloat16 [8192, 2048], P('blk', 'req'), may hold values from -6 to 6
- long_v: bfloat16 [8192, 2048], P('blk', 'req'), may hold values from -6 to 6
- short_q: bfloat16 [4096, 2048], P('blk', 'req'), may hold values from -6 to 6
- short_k: bfloat16 [4096, 2048], P('blk', 'req'), may hold values from -6 to 6
- short_v: bfloat16 [4096, 2048], P('blk', 'req'), may hold values from -6 to 6
- short_seg: int32 [8, 512], P('blk'), may hold values from 0 to 15, never falling along the last dimension, each value on 1 to 96 neighbouring positions
- pool_kv: bfloat16 [512, 2, 16, 2048], P('blk', None, None, 'req'), may hold values from -6 to 6
- page_table: int32 [8, 16, 4], replicated, may hold values from 0 to 511, as said below
- w_out: bfloat16 [2048, 2048], replicated, may hold values from -0.125 to 0.125
Outputs:
- long_out: bfloat16 [8192, 2048], P(('blk', 'req'))
- short_out: bfloat16 [4096, 2048], P(('blk', 'req'))
The draws below stay inside these ranges and needn't reach their ends.
Inputs may be any that keep to these rules, and one draw needn't show every extreme that they name: `short_seg`: along each pack the request numbers never fall, and each of the 16 requests has 1 to 96 tokens, one of them exactly 96. `page_table`: entry [b, s, j] is o * 64 + i for page i of the pool rows held by index o of blk; for every pack b and every o exactly 8 of the 64 entries of b name pages of o.
All inputs are finite; a program needn't handle non-finite values.
Results may differ from the reference program's by a relative error of at most 0.015.
Values may be sent and summed in bfloat16 or wider, within the bound.
A program may use at most 128 MiB of HBM per device.

```python
import math
import jax
import jax.numpy as jnp
import numpy as np
from jax import lax

D = 2048
HEADS = 16
HD = 128
PACK = 512
SEGS = 16
SMAX = 96
PPS = 4
PAGE = 16
POOL = 64
LONG = 8192
QW = 2048
SHORT_ROWS = 4096
CAP = 8
N_BLK = 8


def paired(key, row_count):
    key_query, key_keys = jax.random.split(key, 2)
    queries = jnp.clip(1.6 * jax.random.normal(key_query, (row_count, QW), jnp.float32), -6.0, 6.0)
    keys_all = jnp.clip(1.6 * jax.random.normal(key_keys, (row_count, QW), jnp.float32), -6.0, 6.0)
    return (queries, keys_all)


def draw_long_q(key, part):
    return paired(jax.random.fold_in(key, 11), LONG)[0].astype(jnp.bfloat16)


def draw_long_k(key, part):
    return paired(jax.random.fold_in(key, 11), LONG)[1].astype(jnp.bfloat16)


def draw_short_q(key, part):
    return paired(jax.random.fold_in(key, 23), SHORT_ROWS)[0].astype(jnp.bfloat16)


def draw_short_k(key, part):
    return paired(jax.random.fold_in(key, 23), SHORT_ROWS)[1].astype(jnp.bfloat16)


def draw_page_table(key, part):
    entries = SEGS * PPS
    blocks = entries // CAP
    key_perm, key_local = jax.random.split(jax.random.fold_in(key, 37))
    repeated = jnp.tile(jnp.arange(blocks, dtype=jnp.int32), CAP)
    owners = jax.vmap(lambda one_key: jax.random.permutation(one_key, repeated))(jax.random.split(key_perm, blocks))
    places = jax.random.randint(key_local, (blocks, entries), 0, POOL, dtype=jnp.int32)
    is_last = owners[0] == blocks - 1
    first_last = is_last & (jnp.cumsum(is_last.astype(jnp.int32)) == 1)
    is_first = owners[0] == 0
    first_first = is_first & (jnp.cumsum(is_first.astype(jnp.int32)) == 1)
    row_zero = jnp.where(first_last, POOL - 1, jnp.where(first_first, 0, places[0]))
    places = places.at[0].set(row_zero)
    return (owners * POOL + places).reshape(blocks, SEGS, PPS).astype(jnp.int32)


def levels(rng, dims, cuts, least, largest):
    gain = 1.0
    for axis_at, parts in cuts:
        heights = jax.random.uniform(jax.random.fold_in(jax.random.fold_in(rng, 6), axis_at), (parts,), jnp.float32, least / len(cuts), largest / len(cuts))
        gain = gain * jnp.repeat(jnp.exp(heights), dims[axis_at] // parts).reshape((-1,) + (1,) * (len(dims) - 1 - axis_at))
    return gain


def split_up(count, total, most, slope):
    portions = [(1 << 20) // math.isqrt(grade ** slope) + 1 for grade in range(2, count + 1)]
    rest, given = total - most - (count - 1), [1] * (count - 1)
    while rest > 0:
        free = [i for i in range(count - 1) if given[i] < most]
        whole, left = sum([portions[i] for i in free]), rest
        for i in free:
            extra = min(most - given[i], max(1, left * portions[i] // whole), rest)
            given[i] = given[i] + extra
            rest = rest - extra
    return np.array([most] + given)


def uneven(own_key, count, total, bound, slope):
    if count == 2:
        one = jax.random.randint(own_key, (), max(1, total - bound), min(bound, total - 1) + 1)
        return jnp.stack([one, total - one])
    tallies = jnp.asarray(split_up(count, total, bound, slope), jnp.int32)
    twos = (count - 1) // 2
    source_of, receiver = tallies[1:1 + 2 * twos:2], tallies[2:2 + 2 * twos:2]
    slack = jnp.minimum(source_of - 1, bound - receiver)
    moved = jax.random.randint(jax.random.fold_in(own_key, 1), (twos,), 0, 1 << 20) % (slack + 1)
    tallies = tallies.at[1:1 + 2 * twos:2].set(source_of - moved).at[2:2 + 2 * twos:2].set(receiver + moved)
    return tallies[jax.random.permutation(jax.random.fold_in(own_key, 2), count)]


def centred(own_key, dims, deviation, most, cuts=(), kind=jnp.bfloat16):
    values = deviation * jax.random.normal(own_key, dims, jnp.float32)
    if cuts:
        values = values * levels(own_key, dims, cuts, -0.22, 0.18)
    return jnp.clip(values, -most, most).astype(kind)


def setup_inputs(seed: int = 0) -> dict:
    arg_keys = jax.random.split(jax.random.key(seed), 11)
    return {
        "long_q": draw_long_q(jax.random.fold_in(arg_keys[10], 71), 0),
        "long_k": draw_long_k(jax.random.fold_in(arg_keys[10], 71), 0),
        "long_v": centred(arg_keys[2], (LONG, QW), 1.0, 6.0, ((0, 8), (1, 4))),
        "short_q": draw_short_q(jax.random.fold_in(arg_keys[10], 71), 0),
        "short_k": draw_short_k(jax.random.fold_in(arg_keys[10], 71), 0),
        "short_v": centred(arg_keys[5], (SHORT_ROWS, QW), 1.0, 6.0, ((0, 8), (1, 4))),
        "short_seg": jax.vmap(lambda own: jnp.searchsorted(jnp.cumsum(uneven(own, SEGS, PACK, SMAX, 2)), jnp.arange(PACK), side="right"))(jax.random.split(arg_keys[6], N_BLK)).reshape((N_BLK, PACK)).astype(jnp.int32),
        "pool_kv": centred(arg_keys[7], (N_BLK * POOL, 2, PAGE, QW), 1.6, 6.0, ((0, 8), (3, 4))),
        "page_table": draw_page_table(jax.random.fold_in(arg_keys[10], 71), 0),
        "w_out": centred(arg_keys[9], (QW, D), QW ** -0.5, 0.125),
    }


very_negative = -1e30


def reference(long_q, long_k, long_v, short_q, short_k, short_v, short_seg, pool_kv, page_table, w_out):
    scale = HD ** -0.5
    block_rows = math.gcd(LONG, 1024)
    block_count = LONG // block_rows
    query_heads = long_q.reshape(block_count, block_rows, HEADS, HD)
    key_heads = long_k.reshape(block_count, block_rows, HEADS, HD)
    value_heads = long_v.reshape(block_count, block_rows, HEADS, HD)

    def query_block(block_num):
        queries = lax.dynamic_index_in_dim(query_heads, block_num, 0, keepdims=False).astype(jnp.float32)
        query_pos = block_num * block_rows + jnp.arange(block_rows, dtype=jnp.int32)

        def key_step(key_num, state_now):
            acc_sum, run_max, run_total = state_now
            keys_now = lax.dynamic_index_in_dim(key_heads, key_num, 0, keepdims=False).astype(jnp.float32)
            values_now = lax.dynamic_index_in_dim(value_heads, key_num, 0, keepdims=False).astype(jnp.float32)
            scores = jnp.einsum("qhd,khd->hqk", queries, keys_now) * scale
            key_pos = key_num * block_rows + jnp.arange(block_rows, dtype=jnp.int32)
            allowed = (key_pos[None, :] <= query_pos[:, None])[None]
            scores = jnp.where(allowed, scores, very_negative)
            new_max = jnp.maximum(run_max, jnp.max(scores, axis=-1))
            weights = jnp.where(allowed, jnp.exp(scores - new_max[..., None]), 0.0)
            factor = jnp.exp(run_max - new_max)
            run_total = run_total * factor + jnp.sum(weights, axis=-1)
            rounded = weights.astype(jnp.bfloat16).astype(jnp.float32)
            acc_sum = acc_sum * factor[..., None] + jnp.einsum("hqk,khd->hqd", rounded, values_now)
            return acc_sum, new_max, run_total

        init = (jnp.zeros((HEADS, block_rows, HD), jnp.float32),
                jnp.full((HEADS, block_rows), very_negative, jnp.float32),
                jnp.zeros((HEADS, block_rows), jnp.float32))
        acc_sum, run_max, run_total = lax.fori_loop(jnp.int32(0), block_num + 1, key_step, init)
        merged = acc_sum / run_total[..., None]
        return merged.transpose(1, 0, 2).reshape(block_rows, QW).astype(jnp.bfloat16)

    long_attn = lax.map(query_block, jnp.arange(block_count, dtype=jnp.int32)).reshape(LONG, QW)

    cache_len = SEGS * PPS * PAGE

    def pack_block(block_num):
        page_rows = lax.dynamic_index_in_dim(page_table, block_num, 0, keepdims=False).reshape(SEGS * PPS)
        fetched = pool_kv[page_rows]
        cache_keys = fetched[:, 0].reshape(cache_len, QW)
        cache_values = fetched[:, 1].reshape(cache_len, QW)
        first_row = (block_num * PACK).astype(jnp.int32)
        queries = lax.dynamic_slice_in_dim(short_q, first_row, PACK, 0)
        keys_new = lax.dynamic_slice_in_dim(short_k, first_row, PACK, 0)
        values_new = lax.dynamic_slice_in_dim(short_v, first_row, PACK, 0)
        segment = lax.dynamic_index_in_dim(short_seg, block_num, 0, keepdims=False)
        key_rows = jnp.concatenate([cache_keys, keys_new], 0).astype(jnp.float32).reshape(cache_len + PACK, HEADS, HD)
        value_rows = jnp.concatenate([cache_values, values_new], 0).astype(jnp.float32).reshape(cache_len + PACK, HEADS, HD)
        query_rows = queries.astype(jnp.float32).reshape(PACK, HEADS, HD)
        positions = jnp.arange(PACK, dtype=jnp.int32)
        key_seg = jnp.concatenate([jnp.arange(cache_len, dtype=jnp.int32) // (PPS * PAGE), segment.astype(jnp.int32)])
        key_pos = jnp.concatenate([jnp.full((cache_len,), -1, jnp.int32), positions])
        allowed = ((key_seg[None, :] == segment[:, None]) & (key_pos[None, :] <= positions[:, None]))[None]
        scores = jnp.einsum("qhd,khd->hqk", query_rows, key_rows) * scale
        scores = jnp.where(allowed, scores, very_negative)
        row_max = jnp.max(scores, axis=-1)
        weights = jnp.where(allowed, jnp.exp(scores - row_max[..., None]), 0.0)
        total = jnp.sum(weights, axis=-1)
        rounded = weights.astype(jnp.bfloat16).astype(jnp.float32)
        numer = jnp.einsum("hqk,khd->hqd", rounded, value_rows)
        merged = numer / total[..., None]
        return merged.transpose(1, 0, 2).reshape(PACK, QW).astype(jnp.bfloat16)

    short_attn = lax.map(pack_block, jnp.arange(N_BLK, dtype=jnp.int32)).reshape(N_BLK * PACK, QW)
    long_out = jnp.dot(long_attn, w_out, preferred_element_type=jnp.float32).astype(jnp.bfloat16)
    short_out = jnp.dot(short_attn, w_out, preferred_element_type=jnp.float32).astype(jnp.bfloat16)
    return long_out, short_out
```

```python
import functools

import jax
import jax.numpy as jnp
from jax import lax
from jax.experimental import pallas as pl
from jax.experimental.pallas import tpu as pltpu
from jax.sharding import PartitionSpec as P

HD = 128
PPS = 4
EXP2_SCALE = HD ** -0.5 * 1.4426950408889634
VERY_NEGATIVE = -1e30
MESH = pl.DeviceIdType.MESH


def lane_sum(x):
    total = x[:, :128]
    for at in range(128, x.shape[1], 128):
        total = total + x[:, at:at + 128]
    return total


def scores_of(q, k):
    return lax.dot_general(q, k, (((1,), (1,)), ((), ())), preferred_element_type=jnp.float32)


def kernel(N, RN, H, G, long_q, long_k, long_v, pages_out, sq, sk, sv, q_seg, k_seg,
           l_out, s_out, kbuf, vbuf, qbuf, obuf, pbuf, sbuf,
           kv_send, kv_recv, fwd_send, q_send, q_recv, p_send, p_recv,
           o_send, o_recv, s_send, s_recv):
    d = lax.axis_index("blk")
    req = lax.axis_index("req")
    c, p = d // G, d % G
    R = kbuf.shape[1]
    rr = R // RN
    srows = sbuf.shape[0] // RN
    m_d = (c % 2) * (G - 1 - 2 * p) + p
    total = N * RN
    me = d * RN + req

    barrier = pltpu.get_barrier_semaphore()

    @pl.loop(1, total)
    def _(k):
        other = (me + k) % total
        pl.semaphore_signal(barrier, inc=1, device_id=(other // RN, other % RN), device_id_type=MESH)

    pl.semaphore_wait(barrier, total - 1)

    def head_cols(h):
        return pl.ds(pl.multiple_of(h * HD, HD), HD)

    def kv_copy(k, which):
        h = (c + k) % H
        src = (long_k, long_v)[which].at[:, head_cols(h)]
        dst = (kbuf, vbuf)[which].at[d]
        if k == 0:
            return pltpu.make_async_copy(src, dst, kv_recv.at[which, d])
        return pltpu.make_async_remote_copy(
            src, dst, kv_send.at[which, k], kv_recv.at[which, d],
            device_id=(h * G + p, req), device_id_type=MESH)

    def q_copy(k):
        h = (c + k) % H
        return pltpu.make_async_remote_copy(
            long_q.at[:, head_cols(h)], qbuf.at[c], q_send.at[k], q_recv.at[c],
            device_id=(h * G + m_d, req), device_id_type=MESH)

    q_stays = m_d == p

    for k in list(range(1, H)) + [0]:
        kv_copy(k, 0).start()
        if k == 0:
            @pl.when(q_stays)
            def _():
                pltpu.make_async_copy(long_q.at[:, head_cols(c)], qbuf.at[c], q_recv.at[c]).start()

            @pl.when(jnp.logical_not(q_stays))
            def _():
                q_copy(0).start()
        else:
            q_copy(k).start()
        kv_copy(k, 1).start()

    def page_copy(k):
        other = (d + k) % N
        if k == 0:
            return pltpu.make_async_copy(pages_out.at[d], pbuf.at[d], p_recv.at[d])
        return pltpu.make_async_remote_copy(
            pages_out.at[other], pbuf.at[d], p_send.at[k], p_recv.at[d],
            device_id=(other, req), device_id_type=MESH)

    for k in range(N):
        page_copy(k).start()

    def arrived(buf, b, sem):
        pltpu.make_async_copy(buf.at[b], buf.at[b], sem).wait()

    def fwd_copy(j, k, which):
        buf = (kbuf, vbuf)[which]
        b = j * G + p
        return pltpu.make_async_remote_copy(
            buf.at[b], buf.at[b], fwd_send.at[which, j, k], kv_recv.at[which, b],
            device_id=(c * G + (p + k) % G, req), device_id_type=MESH)

    def out_copy(j, b, r):
        dst = l_out.at[:, head_cols(req * H + c)]
        return pltpu.make_async_remote_copy(
            obuf.at[j, pl.ds(r * rr, rr)], dst, o_send.at[j, r], o_recv.at[req * H + c],
            device_id=(b, r), device_id_type=MESH)

    tq = min(256, R)

    def step(state, q, k, v, mask):
        m, l, acc = state
        s = scores_of(q, k)
        if mask is not None:
            s = jnp.where(mask, s, VERY_NEGATIVE)
        new = jnp.maximum(m, jnp.max(s, axis=1, keepdims=True))
        w = jnp.exp2((s - new) * EXP2_SCALE)
        f = jnp.exp2((m - new) * EXP2_SCALE)
        l = l * f + lane_sum(w)
        acc = acc * f + jnp.dot(w.astype(jnp.bfloat16), v, preferred_element_type=jnp.float32)
        return new, l, acc

    def empty(rows):
        return (jnp.full((rows, 1), VERY_NEGATIVE, jnp.float32),
                jnp.zeros((rows, HD), jnp.float32), jnp.zeros((rows, HD), jnp.float32))

    def finish(state):
        return (state[2] / jnp.sum(state[1], axis=1, keepdims=True)).astype(jnp.bfloat16)

    def block_of(j):
        return j * G + (j % 2) * (G - 1 - 2 * p) + p

    @pl.loop(0, H)
    def _(j):
        b = block_of(j)
        mine = j * G + p
        for which, buf in ((0, kbuf), (1, vbuf)):
            arrived(buf, mine, kv_recv.at[which, mine])
            for k in range(1, G):
                fwd_copy(j, k, which).start()
        for k in range(1, G):
            theirs = j * G + (p + k) % G
            for which, buf in ((0, kbuf), (1, vbuf)):
                arrived(buf, theirs, kv_recv.at[which, theirs])
        arrived(qbuf, j, q_recv.at[j])
        for t in range(R // tq):
            rows = pl.ds(t * tq, tq)
            q = qbuf[j, rows, :]
            keys = (t + 1) * tq
            mask = (lax.broadcasted_iota(jnp.int32, (tq, keys), 1)
                    <= lax.broadcasted_iota(jnp.int32, (tq, keys), 0) + t * tq)
            state = step(empty(tq), q, kbuf[b, pl.ds(0, keys), :], vbuf[b, pl.ds(0, keys), :], mask)
            state = lax.fori_loop(
                0, b, lambda i, st: step(st, q, kbuf[i], vbuf[i], None), state)
            obuf[j, rows, :] = finish(state)
        for r in range(RN):
            here = jnp.logical_and(b == d, req == r)

            @pl.when(here)
            def _():
                pltpu.make_async_copy(
                    obuf.at[j, pl.ds(r * rr, rr)], l_out.at[:, head_cols(req * H + c)],
                    o_recv.at[req * H + c]).start()

            @pl.when(jnp.logical_not(here))
            def _():
                out_copy(j, b, r).start()

    for k in range(N):
        arrived(pbuf, (d + k) % N, p_recv.at[(d + k) % N])

    cache_len = k_seg.shape[1] - sk.shape[0]
    pack = sbuf.shape[0]
    ts = min(256, pack)

    @pl.loop(0, H)
    def _(h):
        cols = head_cols(h)
        ck = pbuf[:, :, 0, :, cols].reshape(cache_len, HD)
        cv = pbuf[:, :, 1, :, cols].reshape(cache_len, HD)
        for t in range(pack // ts):
            rows = pl.ds(t * ts, ts)
            keys = (t + 1) * ts
            q = sq[rows, cols]
            seg = q_seg[rows, :]
            own = jnp.logical_and(
                k_seg[:, pl.ds(cache_len, keys)] == seg,
                lax.broadcasted_iota(jnp.int32, (ts, keys), 1)
                <= lax.broadcasted_iota(jnp.int32, (ts, keys), 0) + t * ts)
            state = step(empty(ts), q, sk[pl.ds(0, keys), cols], sv[pl.ds(0, keys), cols], own)
            state = step(state, q, ck, cv, k_seg[:, pl.ds(0, cache_len)] == seg)
            sbuf[rows, cols] = finish(state)

    def short_copy(k):
        r = (req + k) % RN
        W = sbuf.shape[1]
        src = sbuf.at[pl.ds(pl.multiple_of(r * srows, srows), srows)]
        dst = s_out.at[:, pl.ds(pl.multiple_of(req * W, W), W)]
        if k == 0:
            return pltpu.make_async_copy(src, dst, s_recv.at[req])
        return pltpu.make_async_remote_copy(
            src, dst, s_send.at[k], s_recv.at[req], device_id=(d, r), device_id_type=MESH)

    for k in range(RN):
        short_copy(k).start()
    for k in range(RN):
        r = (req + k) % RN
        W = sbuf.shape[1]
        dst = s_out.at[:, pl.ds(pl.multiple_of(r * W, W), W)]
        pltpu.make_async_copy(dst, dst, s_recv.at[r]).wait()

    @pl.loop(0, RN * H)
    def _(i):
        dst = l_out.at[:, head_cols(i)]
        pltpu.make_async_copy(dst, dst, o_recv.at[i]).wait()

    for k in range(1, RN):
        short_copy(k).wait_send()
    for k in range(1, N):
        page_copy(k).wait_send()
    for k in range(1, H):
        kv_copy(k, 0).wait_send()
        kv_copy(k, 1).wait_send()
        q_copy(k).wait_send()

    @pl.when(jnp.logical_not(q_stays))
    def _():
        q_copy(0).wait_send()

    @pl.loop(0, H)
    def _(j):
        b = block_of(j)
        for k in range(1, G):
            fwd_copy(j, k, 0).wait_send()
            fwd_copy(j, k, 1).wait_send()
        for r in range(RN):
            @pl.when(jnp.logical_not(jnp.logical_and(b == d, req == r)))
            def _():
                out_copy(j, b, r).wait_send()


def per_device(
    long_q, long_k, long_v, short_q, short_k, short_v, short_seg, pool_kv, page_table, w_out
):
    N = lax.axis_size("blk")
    RN = lax.axis_size("req")
    d = lax.axis_index("blk")
    R, W = long_q.shape
    H = W // HD
    G = N // H
    pack = short_q.shape[0]
    pool_pages = pool_kv.shape[0]
    page_len = pool_kv.shape[2]
    table = page_table.reshape(N, -1)
    entries = table.shape[1]
    cap = entries // N
    owners = table // pool_pages
    places = table % pool_pages
    wanted = owners == d
    ranks = jnp.cumsum(wanted.astype(jnp.int32), axis=1) - 1
    picked = wanted[:, :, None] & (
        ranks[:, :, None] == jnp.arange(cap, dtype=jnp.int32)[None, None, :]
    )
    send_places = jnp.sum(jnp.where(picked, places[:, :, None], 0), axis=1)
    outgoing = pool_kv[send_places.reshape(-1)].reshape(N, cap, 2, page_len, W)
    my_owners = lax.dynamic_index_in_dim(owners, d, 0, keepdims=False)
    order = jnp.arange(entries, dtype=jnp.int32)
    before = (my_owners[None, :] == my_owners[:, None]) & (order[None, :] < order[:, None])
    slots = my_owners * cap + jnp.sum(before.astype(jnp.int32), axis=1)
    slot_seg = jnp.sum(jnp.where(slots[:, None] == order[None, :], (order // PPS)[:, None], 0), axis=0)
    segment = short_seg[0]
    k_seg = jnp.concatenate([jnp.repeat(slot_seg, page_len), segment])[None, :]
    q_seg = segment[:, None]

    DMA = pltpu.SemaphoreType.DMA
    vmem = pl.BlockSpec(memory_space=pltpu.VMEM)
    anywhere = pl.BlockSpec(memory_space=pl.ANY)
    bf16 = jnp.bfloat16
    l_attn, s_attn = pl.pallas_call(
        functools.partial(kernel, N, RN, H, G),
        out_shape=(jax.ShapeDtypeStruct((R // RN, W * RN), bf16),
                   jax.ShapeDtypeStruct((pack // RN, W * RN), bf16)),
        in_specs=[anywhere] * 4 + [vmem] * 5,
        out_specs=(anywhere, anywhere),
        scratch_shapes=[
            pltpu.VMEM((N, R, HD), bf16), pltpu.VMEM((N, R, HD), bf16),
            pltpu.VMEM((H, R, HD), bf16), pltpu.VMEM((H, R, HD), bf16),
            pltpu.VMEM((N, cap, 2, page_len, W), bf16), pltpu.VMEM((pack, W), bf16),
            DMA((2, H)), DMA((2, N)), DMA((2, H, G)), DMA((H,)), DMA((H,)),
            DMA((N,)), DMA((N,)), DMA((H, RN)), DMA((RN * H,)), DMA((RN,)), DMA((RN,)),
        ],
        compiler_params=pltpu.CompilerParams(
            collective_id=0, has_side_effects=True, vmem_limit_bytes=52 * 2**20),
    )(long_q, long_k, long_v, outgoing, short_q, short_k, short_v, q_seg, k_seg)
    return (jnp.dot(l_attn, w_out, preferred_element_type=jnp.float32).astype(bf16),
            jnp.dot(s_attn, w_out, preferred_element_type=jnp.float32).astype(bf16))


def solution(mesh):
    placed = (
        P("blk", "req"),
        P("blk", "req"),
        P("blk", "req"),
        P("blk", "req"),
        P("blk", "req"),
        P("blk", "req"),
        P("blk", None),
        P("blk", None, None, "req"),
        P(),
        P(),
    )
    return jax.shard_map(
        per_device,
        mesh=mesh,
        in_specs=placed,
        out_specs=(P(("blk", "req"), None), P(("blk", "req"), None)),
        check_vma=False,
    )
```

```python
import functools

import jax
import jax.numpy as jnp
from jax import lax
from jax.experimental import pallas as pl
from jax.experimental.pallas import tpu as pltpu
from jax.sharding import PartitionSpec as P

HD = 128
PPS = 4
EXP2_SCALE = HD ** -0.5 * 1.4426950408889634
VERY_NEGATIVE = -1e30
MESH = pl.DeviceIdType.MESH


def lane_sum(x):
    total = x[:, :128]
    for at in range(128, x.shape[1], 128):
        total = total + x[:, at:at + 128]
    return total


def scores_of(q, k):
    return lax.dot_general(q, k, (((1,), (1,)), ((), ())), preferred_element_type=jnp.float32)


def kernel(N, RN, H, G, long_q, long_k, long_v, pages_out, short_q, short_k, short_v, w_hbm, q_seg, k_seg,
           long_res, short_res, kbuf, vbuf, qbuf, obuf, pbuf, sbuf, sq, sk, sv, w_out, l_out, s_out,
           m_keep, l_keep, a_keep, local_sem, kv_send, kv_recv, fwd_send, q_send, q_recv, p_send, p_recv,
           o_send, o_recv, s_send, s_recv):
    d = lax.axis_index("blk")
    req = lax.axis_index("req")
    c, p = d // G, d % G
    R = kbuf.shape[1]
    rr = R // RN
    srows = sbuf.shape[0] // RN
    m_d = (c % 2) * (G - 1 - 2 * p) + p
    total = N * RN
    me = d * RN + req

    def local_copies():
        return [pltpu.make_async_copy(src, dst, local_sem.at[i]) for i, (src, dst) in enumerate(
            ((short_q, sq), (short_k, sk), (short_v, sv), (w_hbm, w_out)))]

    for copy in local_copies():
        copy.start()

    barrier = pltpu.get_barrier_semaphore()

    @pl.loop(1, total)
    def _(k):
        other = (me + k) % total
        pl.semaphore_signal(barrier, inc=1, device_id=(other // RN, other % RN), device_id_type=MESH)

    pl.semaphore_wait(barrier, total - 1)

    def head_cols(h):
        return pl.ds(pl.multiple_of(h * HD, HD), HD)

    def kv_copy(k, which):
        h = (c + k) % H
        src = (long_k, long_v)[which].at[:, head_cols(h)]
        dst = (kbuf, vbuf)[which].at[d]
        if k == 0:
            return pltpu.make_async_copy(src, dst, kv_recv.at[which, d])
        return pltpu.make_async_remote_copy(
            src, dst, kv_send.at[which, k], kv_recv.at[which, d],
            device_id=(h * G + p, req), device_id_type=MESH)

    def q_copy(k):
        h = (c + k) % H
        return pltpu.make_async_remote_copy(
            long_q.at[:, head_cols(h)], qbuf.at[c], q_send.at[k], q_recv.at[c],
            device_id=(h * G + m_d, req), device_id_type=MESH)

    q_stays = m_d == p

    for k in list(range(1, H)) + [0]:
        kv_copy(k, 0).start()
        if k == 0:
            @pl.when(q_stays)
            def _():
                pltpu.make_async_copy(long_q.at[:, head_cols(c)], qbuf.at[c], q_recv.at[c]).start()

            @pl.when(jnp.logical_not(q_stays))
            def _():
                q_copy(0).start()
        else:
            q_copy(k).start()
        kv_copy(k, 1).start()

    def page_copy(k):
        other = (d + k) % N
        if k == 0:
            return pltpu.make_async_copy(pages_out.at[d], pbuf.at[d], p_recv.at[d])
        return pltpu.make_async_remote_copy(
            pages_out.at[other], pbuf.at[d], p_send.at[k], p_recv.at[d],
            device_id=(other, req), device_id_type=MESH)

    def arrived(buf, b, sem):
        pltpu.make_async_copy(buf.at[b], buf.at[b], sem).wait()

    def fwd_copy(j, k, which):
        buf = (kbuf, vbuf)[which]
        b = j * G + p
        return pltpu.make_async_remote_copy(
            buf.at[b], buf.at[b], fwd_send.at[which, j, k], kv_recv.at[which, b],
            device_id=(c * G + (p + k) % G, req), device_id_type=MESH)

    def out_copy(j, b, r):
        dst = l_out.at[:, head_cols(req * H + c)]
        return pltpu.make_async_remote_copy(
            obuf.at[j, pl.ds(r * rr, rr)], dst, o_send.at[j, r], o_recv.at[req * H + c],
            device_id=(b, r), device_id_type=MESH)

    tq = min(256, R)

    def step(state, q, k, v, mask):
        m, l, acc = state
        s = scores_of(q, k)
        if mask is not None:
            s = jnp.where(mask, s, VERY_NEGATIVE)
        new = jnp.maximum(m, jnp.max(s, axis=1, keepdims=True))
        w = jnp.exp2((s - new) * EXP2_SCALE)
        f = jnp.exp2((m - new) * EXP2_SCALE)
        l = l * f + lane_sum(w)
        acc = acc * f + jnp.dot(w.astype(jnp.bfloat16), v, preferred_element_type=jnp.float32)
        return new, l, acc

    def empty(rows):
        return (jnp.full((rows, 1), VERY_NEGATIVE, jnp.float32),
                jnp.zeros((rows, HD), jnp.float32), jnp.zeros((rows, HD), jnp.float32))

    def finish(state):
        return (state[2] / jnp.sum(state[1], axis=1, keepdims=True)).astype(jnp.bfloat16)

    def block_of(j):
        return j * G + (j % 2) * (G - 1 - 2 * p) + p

    cache_len = k_seg.shape[1] - sk.shape[0]
    pack = sbuf.shape[0]
    ts = min(256, pack)

    for copy in local_copies()[:3]:
        copy.wait()

    @pl.loop(0, H)
    def _(h):
        cols = head_cols(h)
        for t in range(pack // ts):
            rows = pl.ds(t * ts, ts)
            keys = (t + 1) * ts
            own = jnp.logical_and(
                k_seg[:, pl.ds(cache_len, keys)] == q_seg[rows, :],
                lax.broadcasted_iota(jnp.int32, (ts, keys), 1)
                <= lax.broadcasted_iota(jnp.int32, (ts, keys), 0) + t * ts)
            m, l, acc = step(
                empty(ts), sq[rows, cols], sk[pl.ds(0, keys), cols], sv[pl.ds(0, keys), cols], own)
            m_keep[h, rows, :] = jnp.broadcast_to(m, (ts, HD))
            l_keep[h, rows, :] = l
            a_keep[h, rows, :] = acc

    @pl.loop(0, H)
    def _(j):
        b = block_of(j)
        mine = j * G + p
        for which, buf in ((0, kbuf), (1, vbuf)):
            arrived(buf, mine, kv_recv.at[which, mine])
            for k in range(1, G):
                fwd_copy(j, k, which).start()
        for k in range(1, G):
            theirs = j * G + (p + k) % G
            for which, buf in ((0, kbuf), (1, vbuf)):
                arrived(buf, theirs, kv_recv.at[which, theirs])
        arrived(qbuf, j, q_recv.at[j])

        @pl.when(j == 0)
        def _():
            for k in range(N):
                page_copy(k).start()

        states = []
        for t in range(R // tq):
            keys = (t + 1) * tq
            mask = (lax.broadcasted_iota(jnp.int32, (tq, keys), 1)
                    <= lax.broadcasted_iota(jnp.int32, (tq, keys), 0) + t * tq)
            states.append(step(
                empty(tq), qbuf[j, pl.ds(t * tq, tq), :],
                kbuf[b, pl.ds(0, keys), :], vbuf[b, pl.ds(0, keys), :], mask))

        def one_block(i, now):
            k, v = kbuf[i], vbuf[i]
            return tuple(
                step(now[t], qbuf[j, pl.ds(t * tq, tq), :], k, v, None) for t in range(R // tq))

        states = lax.fori_loop(0, b, one_block, tuple(states))
        for t in range(R // tq):
            obuf[j, pl.ds(t * tq, tq), :] = finish(states[t])
        for r in range(RN):
            here = jnp.logical_and(b == d, req == r)

            @pl.when(here)
            def _():
                pltpu.make_async_copy(
                    obuf.at[j, pl.ds(r * rr, rr)], l_out.at[:, head_cols(req * H + c)],
                    o_recv.at[req * H + c]).start()

            @pl.when(jnp.logical_not(here))
            def _():
                out_copy(j, b, r).start()

    for k in range(N):
        arrived(pbuf, (d + k) % N, p_recv.at[(d + k) % N])

    @pl.loop(0, H)
    def _(h):
        cols = head_cols(h)
        ck = pbuf[:, :, 0, :, cols].reshape(cache_len, HD)
        cv = pbuf[:, :, 1, :, cols].reshape(cache_len, HD)
        for t in range(pack // ts):
            rows = pl.ds(t * ts, ts)
            state = (m_keep[h, rows, :][:, :1], l_keep[h, rows, :], a_keep[h, rows, :])
            state = step(
                state, sq[rows, cols], ck, cv, k_seg[:, pl.ds(0, cache_len)] == q_seg[rows, :])
            sbuf[rows, cols] = finish(state)

    def short_copy(k):
        r = (req + k) % RN
        W = sbuf.shape[1]
        src = sbuf.at[pl.ds(pl.multiple_of(r * srows, srows), srows)]
        dst = s_out.at[:, pl.ds(pl.multiple_of(req * W, W), W)]
        if k == 0:
            return pltpu.make_async_copy(src, dst, s_recv.at[req])
        return pltpu.make_async_remote_copy(
            src, dst, s_send.at[k], s_recv.at[req], device_id=(d, r), device_id_type=MESH)

    for k in range(RN):
        short_copy(k).start()
    local_copies()[3].wait()
    WHOLE = l_out.shape[1]
    nt = min(512, WHOLE)

    def project(attn, result):
        @pl.loop(0, WHOLE // nt)
        def _(n):
            cols = pl.ds(pl.multiple_of(n * nt, nt), nt)
            result[:, cols] = jnp.dot(
                attn[...], w_out[:, cols], preferred_element_type=jnp.float32
            ).astype(jnp.bfloat16)

    @pl.loop(0, RN * H)
    def _(i):
        dst = l_out.at[:, head_cols(i)]
        pltpu.make_async_copy(dst, dst, o_recv.at[i]).wait()

    project(l_out, long_res)

    for k in range(RN):
        r = (req + k) % RN
        W = sbuf.shape[1]
        dst = s_out.at[:, pl.ds(pl.multiple_of(r * W, W), W)]
        pltpu.make_async_copy(dst, dst, s_recv.at[r]).wait()

    project(s_out, short_res)

    for k in range(1, RN):
        short_copy(k).wait_send()
    for k in range(1, N):
        page_copy(k).wait_send()
    for k in range(1, H):
        kv_copy(k, 0).wait_send()
        kv_copy(k, 1).wait_send()
        q_copy(k).wait_send()

    @pl.when(jnp.logical_not(q_stays))
    def _():
        q_copy(0).wait_send()

    @pl.loop(0, H)
    def _(j):
        b = block_of(j)
        for k in range(1, G):
            fwd_copy(j, k, 0).wait_send()
            fwd_copy(j, k, 1).wait_send()
        for r in range(RN):
            @pl.when(jnp.logical_not(jnp.logical_and(b == d, req == r)))
            def _():
                out_copy(j, b, r).wait_send()


def per_device(
    long_q, long_k, long_v, short_q, short_k, short_v, short_seg, pool_kv, page_table, w_out
):
    N = lax.axis_size("blk")
    RN = lax.axis_size("req")
    d = lax.axis_index("blk")
    R, W = long_q.shape
    H = W // HD
    G = N // H
    pack = short_q.shape[0]
    pool_pages = pool_kv.shape[0]
    page_len = pool_kv.shape[2]
    table = page_table.reshape(N, -1)
    entries = table.shape[1]
    cap = entries // N
    owners = table // pool_pages
    places = table % pool_pages
    wanted = owners == d
    ranks = jnp.cumsum(wanted.astype(jnp.int32), axis=1) - 1
    picked = wanted[:, :, None] & (
        ranks[:, :, None] == jnp.arange(cap, dtype=jnp.int32)[None, None, :]
    )
    send_places = jnp.sum(jnp.where(picked, places[:, :, None], 0), axis=1)
    outgoing = pool_kv[send_places.reshape(-1)].reshape(N, cap, 2, page_len, W)
    my_owners = lax.dynamic_index_in_dim(owners, d, 0, keepdims=False)
    order = jnp.arange(entries, dtype=jnp.int32)
    before = (my_owners[None, :] == my_owners[:, None]) & (order[None, :] < order[:, None])
    slots = my_owners * cap + jnp.sum(before.astype(jnp.int32), axis=1)
    slot_seg = jnp.sum(jnp.where(slots[:, None] == order[None, :], (order // PPS)[:, None], 0), axis=0)
    segment = short_seg[0]
    k_seg = jnp.concatenate([jnp.repeat(slot_seg, page_len), segment])[None, :]
    q_seg = segment[:, None]

    DMA = pltpu.SemaphoreType.DMA
    vmem = pl.BlockSpec(memory_space=pltpu.VMEM)
    anywhere = pl.BlockSpec(memory_space=pl.ANY)
    bf16 = jnp.bfloat16
    return pl.pallas_call(
        functools.partial(kernel, N, RN, H, G),
        out_shape=(jax.ShapeDtypeStruct((R // RN, W * RN), bf16),
                   jax.ShapeDtypeStruct((pack // RN, W * RN), bf16)),
        in_specs=[anywhere] * 8 + [vmem] * 2,
        out_specs=(vmem, vmem),
        scratch_shapes=[
            pltpu.VMEM((N, R, HD), bf16), pltpu.VMEM((N, R, HD), bf16),
            pltpu.VMEM((H, R, HD), bf16), pltpu.VMEM((H, R, HD), bf16),
            pltpu.VMEM((N, cap, 2, page_len, W), bf16), pltpu.VMEM((pack, W), bf16),
            pltpu.VMEM((pack, W), bf16), pltpu.VMEM((pack, W), bf16), pltpu.VMEM((pack, W), bf16),
            pltpu.VMEM(w_out.shape, bf16),
            pltpu.VMEM((R // RN, W * RN), bf16), pltpu.VMEM((pack // RN, W * RN), bf16),
            pltpu.VMEM((H, pack, HD), jnp.float32), pltpu.VMEM((H, pack, HD), jnp.float32),
            pltpu.VMEM((H, pack, HD), jnp.float32), DMA((4,)),
            DMA((2, H)), DMA((2, N)), DMA((2, H, G)), DMA((H,)), DMA((H,)),
            DMA((N,)), DMA((N,)), DMA((H, RN)), DMA((RN * H,)), DMA((RN,)), DMA((RN,)),
        ],
        compiler_params=pltpu.CompilerParams(
            collective_id=0, has_side_effects=True, vmem_limit_bytes=52 * 2**20),
    )(long_q, long_k, long_v, outgoing, short_q, short_k, short_v, w_out, q_seg, k_seg)


def solution(mesh):
    placed = (
        P("blk", "req"),
        P("blk", "req"),
        P("blk", "req"),
        P("blk", "req"),
        P("blk", "req"),
        P("blk", "req"),
        P("blk", None),
        P("blk", None, None, "req"),
        P(),
        P(),
    )
    return jax.shard_map(
        per_device,
        mesh=mesh,
        in_specs=placed,
        out_specs=(P(("blk", "req"), None), P(("blk", "req"), None)),
        check_vma=False,
    )
```
